128 devices in a mesh: mom: 16 (over x, z), band: 8 (over y, core).
Axes of the slice: x: 4, y: 4, z: 4, core: 2. Of those that a mesh axis runs over, the one named last changes fastest.
Arguments:
- ints: bfloat16 [2, 64, 16, 256, 8, 256], P(None, 'mom', None, 'band'), may hold values from -6 to 6
- vir_coef: bfloat16 [64, 2, 256, 256], P('mom'), may hold values from -0.375 to 0.375
- occ_coef: bfloat16 [64, 2, 256, 16], P(None, None, 'band'), may hold values from -0.5 to 0.5
- k4_table: int32 [64, 16], P('mom'), may hold values from 0 to 63, as said below
- band_mask: int32 [64, 256], replicated, may hold values from 0 to 1, as said below
Outputs:
- mo_ints: float32 [2, 64, 16, 16, 8, 256], P(None, None, 'mom', 'band')
The draws below stay inside these ranges and needn't reach their ends.
Inputs may be any that keep to these rules, and one draw needn't show every extreme that they name: `k4_table`: each column of the table is a permutation of the 64 k-points. `band_mask`: each k-point's active window is a leading run of at least 128 slots; k-point 0 uses all 256.
All inputs are finite; a program needn't handle non-finite values.
Results may differ from the reference program's by a relative error of at most 0.0029.
Values may be sent and summed in bfloat16 or wider, within the bound.
No kernel may reach another device: no remote copies, remote signals or barrier semaphores. Data moves between devices by JAX's collectives and lax.ppermute only.
A program may use at most 192 MiB of HBM per device.

```python
import jax
import jax.numpy as jnp
from jax import lax

NAO = 256
NB = 256
NOCC = 16
M = 8
KPTS = 64
K3 = 16


def draw_k4_table(key, part):
    key = jax.random.fold_in(key, 11)
    keys = jax.random.split(key, K3)
    perms = jax.vmap(lambda single: jax.random.permutation(single, KPTS))(keys)
    return perms.T.astype(jnp.int32)


def draw_band_mask(key, part):
    key = jax.random.fold_in(key, 12)
    widths = jax.random.randint(key, (KPTS,), NB // 2, NB + 1)
    widths = widths.at[0].set(NB)
    slots = jnp.arange(NB)
    return (slots[None, :] < widths[:, None]).astype(jnp.int32)


def strengthened(entries, rng, source, target, shards_of, factor):
    owner, partner = [(jnp.arange(entries.shape[axis_at]) // (entries.shape[axis_at] // shards_of)).reshape([-1 if axis == axis_at else 1 for axis in range(entries.ndim)]) for axis_at in (source, target)]
    chosen = jax.random.permutation(rng, shards_of)[partner]
    strong = (owner == chosen) | (owner == (partner + shards_of // 2) % shards_of)
    return jnp.where(strong, factor * entries, entries)


def levels(stream_key, shape, pieces, low, high):
    level = 1.0
    for position, shards_of in pieces:
        heights = jax.random.uniform(jax.random.fold_in(jax.random.fold_in(stream_key, 6), position), (shards_of,), jnp.float32, low / len(pieces), high / len(pieces))
        level = level * jnp.repeat(jnp.exp(heights), shape[position] // shards_of).reshape((-1,) + (1,) * (len(shape) - 1 - position))
    return level


def scatter_about(key, shape, scale, reach, cuts=(), held_as=jnp.bfloat16):
    array = scale * jax.random.normal(key, shape, jnp.float32)
    if cuts:
        array = array * levels(key, shape, cuts, -0.22, 0.18)
    return jnp.clip(array, -reach, reach).astype(held_as)


def noise_with(own_key, extent, width, most, cuts, heavy, dtype=jnp.bfloat16):
    values = width * jax.random.normal(own_key, extent, jnp.float32)
    if cuts:
        values = values * levels(own_key, extent, cuts, -0.22, 0.18)
    return jnp.clip(strengthened(values, jax.random.fold_in(own_key, 3), *heavy), -most, most).astype(dtype)


def setup_inputs(seed: int = 0) -> dict:
    key_of = jax.random.split(jax.random.key(seed), 6)
    ints = scatter_about(key_of[0], (2, KPTS, K3, NAO, M, NAO), 1.0, 6.0, ((1, 16), (3, 8)))
    vir_coef = scatter_about(key_of[1], (KPTS, 2, NAO, NB), NAO ** -0.5, 0.375, ((0, 16),))
    occ_coef = noise_with(key_of[2], (KPTS, 2, NAO, NOCC), NAO ** -0.5, 0.5, ((2, 8),), (2, 3, 8, 2.0))
    k4_table = draw_k4_table(jax.random.fold_in(key_of[5], 71), 0)
    band_mask = draw_band_mask(jax.random.fold_in(key_of[5], 71), 0)
    return dict(ints=ints, vir_coef=vir_coef, occ_coef=occ_coef, k4_table=k4_table, band_mask=band_mask)


def one_block(args):
    block, columns, occ = args
    xr = block[0].astype(jnp.float32)
    xi = block[1].astype(jnp.float32)
    cr = columns[:, 0]
    ci = columns[:, 1]
    form = "tqms,tsb->tqmb"
    yr = jnp.einsum(form, xr, cr) - jnp.einsum(form, xi, ci)
    yi = jnp.einsum(form, xr, ci) + jnp.einsum(form, xi, cr)
    yr = lax.optimization_barrier(yr.astype(jnp.bfloat16)).astype(jnp.float32)
    yi = lax.optimization_barrier(yi.astype(jnp.bfloat16)).astype(jnp.float32)
    occ_real = occ[0].astype(jnp.float32)
    occ_imag = occ[1].astype(jnp.float32)
    second = "tqmb,qa->tamb"
    zr = jnp.einsum(second, yr, occ_real) - jnp.einsum(second, yi, occ_imag)
    zi = jnp.einsum(second, yr, occ_imag) + jnp.einsum(second, yi, occ_real)
    return jnp.stack([zr, zi])


def reference(ints, vir_coef, occ_coef, k4_table, band_mask):
    masked = vir_coef.astype(jnp.float32) * band_mask[:, None, None, :].astype(jnp.float32)

    def per_k2(args):
        block, table_row, occ = args
        columns = masked[table_row]
        return one_block((block, columns, occ))

    result = lax.map(per_k2, (jnp.moveaxis(ints, 1, 0), k4_table, occ_coef))
    return jnp.moveaxis(result, 0, 1)
```

```python
import functools

import jax
import jax.numpy as jnp
from jax import lax
from jax.experimental import pallas as pl
from jax.experimental.pallas import tpu as pltpu
from jax.sharding import PartitionSpec as P

CHUNKS = 2
PAIR_TYPE = jnp.float32
STEP = 8
MIB = 1 << 20


def contract_occupied(coef, ints, first, count):
    def kernel(coef_ref, ints_ref, mine_ref, theirs_ref, wide):
        @pl.when(pl.program_id(1) == 0)
        def _():
            rows = lax.broadcasted_iota(jnp.int32, (256, 32), 0) // 8
            spread = (rows == lax.broadcasted_iota(jnp.int32, (256, 32), 1)).astype(jnp.bfloat16)
            cols = lax.broadcasted_iota(jnp.int32, (64, 512), 1) // 8
            across = (cols == lax.broadcasted_iota(jnp.int32, (64, 512), 0)).astype(jnp.bfloat16)
            tall = jnp.dot(spread, coef_ref[0], preferred_element_type=jnp.float32).astype(jnp.bfloat16)
            full = jnp.dot(tall, across, preferred_element_type=jnp.float32)
            same = (
                lax.broadcasted_iota(jnp.int32, (256, 512), 0) % 8 == lax.broadcasted_iota(jnp.int32, (256, 512), 1) % 8
            )
            wide[...] = jnp.where(same, full, 0.0).astype(jnp.bfloat16)

        for t in range(STEP):
            got = jnp.dot(wide[:, :256], ints_ref[0, 0, t], preferred_element_type=jnp.float32)
            got = got + jnp.dot(wide[:, 256:], ints_ref[1, 0, t], preferred_element_type=jnp.float32)
            for d in range(4):
                mine_ref[d, 0, t] = got[32 * d : 32 * d + 32]
                theirs_ref[d, 0, t] = got[128 + 32 * d : 160 + 32 * d].astype(theirs_ref.dtype)

    block = pl.BlockSpec((4, 1, STEP, 32, 256), lambda k, t: (0, k, t, 0, 0))
    return pl.pallas_call(
        kernel,
        grid=(count, 16 // STEP),
        in_specs=[
            pl.BlockSpec((1, 32, 64), lambda k, t: (k + first, 0, 0)),
            pl.BlockSpec((2, 1, STEP, 256, 256), lambda k, t: (0, k + first, t, 0, 0)),
        ],
        out_specs=[block, block],
        out_shape=[
            jax.ShapeDtypeStruct((4, count, 16, 32, 256), jnp.float32),
            jax.ShapeDtypeStruct((4, count, 16, 32, 256), PAIR_TYPE),
        ],
        scratch_shapes=[pltpu.VMEM((256, 512), jnp.bfloat16)],
        compiler_params=pltpu.CompilerParams(vmem_limit_bytes=40 * MIB),
        cost_estimate=pl.CostEstimate(
            flops=count * 16 * 2 * 256 * 512 * 256, bytes_accessed=count * 16 * 512 * 1024, transcendentals=0
        ),
        name="contract_occupied",
    )(coef, ints)


def contract_virtual(k4, core, mask, held, other, u, out, first, count):
    n = 16 * count

    def kernel(k4_ref, core_ref, mask_ref, held_ref, other_ref, u_ref, *rest):
        out_ref, own, paired, sems = rest[-4:]

        def copies(k):
            at = k4_ref[(k // count) * 4 + first + k % count]
            return (
                pltpu.make_async_copy(held_ref.at[at], own.at[k], sems.at[0, k]),
                pltpu.make_async_copy(other_ref.at[at], paired.at[k], sems.at[1, k]),
            )

        @pl.loop(0, n)
        def _(k):
            for copy in copies(k):
                copy.start()

        even = core_ref[0] == 0

        @pl.loop(0, n)
        def _(k):
            for copy in copies(k):
                copy.wait()
            at = k4_ref[(k // count) * 4 + first + k % count]
            full = u_ref[k // count, k % count]
            high = full.astype(jnp.bfloat16)
            low = (full - high.astype(jnp.float32)).astype(jnp.bfloat16)
            rows = jnp.concatenate([high, low], axis=0)
            a = jnp.dot(rows, own[k], preferred_element_type=jnp.float32)
            b = jnp.dot(rows, paired[k], preferred_element_type=jnp.float32)
            a = a[:32] + a[32:]
            b = b[:32] + b[32:]
            by_real = jnp.where(even, a, b)
            by_imag = jnp.where(even, b, a)
            keep = mask_ref[pl.ds(at, 1), :].astype(jnp.float32)
            real = (by_real[:16] - by_imag[16:]) * keep
            imag = (by_imag[:16] + by_real[16:]) * keep
            out_ref[0, k // count, k % count] = real
            out_ref[1, k // count, k % count] = imag

    whole = pl.BlockSpec(memory_space=pl.ANY)
    args = [k4, core, mask, held, other, u]
    specs = [
        pl.BlockSpec(memory_space=pltpu.SMEM),
        pl.BlockSpec(memory_space=pltpu.SMEM),
        pl.BlockSpec((64, 256), lambda i: (0, 0)),
        whole,
        whole,
        pl.BlockSpec((16, count, 32, 256), lambda i: (0, 0, 0, 0)),
    ]
    alias = {}
    if out is not None:
        args.append(out)
        specs.append(whole)
        alias = {6: 0}
    return pl.pallas_call(
        kernel,
        grid=(1,),
        in_specs=specs,
        out_specs=pl.BlockSpec((2, 16, count, 16, 256), lambda i: (0, 0, first // count, 0, 0)),
        out_shape=jax.ShapeDtypeStruct((2, 16, 4, 16, 256), jnp.float32),
        scratch_shapes=[
            pltpu.VMEM((n, 256, 256), jnp.bfloat16),
            pltpu.VMEM((n, 256, 256), jnp.bfloat16),
            pltpu.SemaphoreType.DMA((2, n)),
        ],
        input_output_aliases=alias,
        compiler_params=pltpu.CompilerParams(vmem_limit_bytes=48 * MIB),
        cost_estimate=pl.CostEstimate(
            flops=n * 2 * 2 * 64 * 256 * 256, bytes_accessed=n * 300 * 1024, transcendentals=0
        ),
        name="contract_virtual",
    )(*args)


def per_device(ints, vir_coef, occ_coef, k4_table, band_mask):
    mom, band = lax.axis_index("mom"), lax.axis_index("band")
    core, y = band % 2, band // 2

    def across(x):
        return lax.ppermute(x, "band", [(i, i ^ 1) for i in range(8)])

    def along(x, d):
        return lax.ppermute(x, "band", [(i, (i // 2 + d) % 4 * 2 + i % 2) for i in range(8)])

    table = lax.all_gather(k4_table, "mom", axis=0, tiled=True)
    k4 = lax.dynamic_index_in_dim(table, mom, axis=1, keepdims=False)
    half = lax.dynamic_index_in_dim(vir_coef, core, axis=1, keepdims=False)
    held = lax.all_gather(half, "mom", axis=0, tiled=True)

    occ = lax.dynamic_slice_in_dim(occ_coef, 4 * mom, 4, axis=0)
    order = (
        4 * ((y + jnp.arange(4)[None, :, None]) % 4)
        + 2 * ((core + jnp.arange(2)[:, None, None]) % 2)
        + jnp.arange(2)[None, None, :]
    ).reshape(16)
    occ = jnp.take(occ, order, axis=3).reshape(4, 2, 32, 8, 2)
    parts = jnp.stack([jnp.stack([occ[:, 0], -occ[:, 1]], 1), jnp.stack([occ[:, 1], occ[:, 0]], 1)], 1)
    coef = parts.transpose(0, 4, 1, 5, 2, 3).reshape(4, 32, 64)

    ints = ints.reshape(2, 4, 16, 256, 256)
    count = 4 // CHUNKS
    sums = []
    for c in range(CHUNKS):
        mine, theirs = contract_occupied(coef, ints, c * count, count)
        sums.append((mine, across(theirs)))
    moved = []
    for mine, got in sums:
        total = [mine[d] + got[d].astype(jnp.float32) for d in range(4)]
        up = along(total[2][:, :8].astype(jnp.bfloat16), 1)
        down = along(total[2][:, 8:].astype(jnp.bfloat16), -1)
        right = jnp.concatenate([total[1][:, :8] + up.astype(jnp.float32), total[1][:, 8:]], axis=1)
        left = jnp.concatenate([total[3][:, :8], total[3][:, 8:] + down.astype(jnp.float32)], axis=1)
        right = along(right.astype(jnp.bfloat16), 1)
        left = along(left.astype(jnp.bfloat16), -1)
        u = total[0] + right.astype(jnp.float32) + left.astype(jnp.float32)
        u = u.transpose(1, 0, 2, 3)
        moved.append(lax.all_to_all(u, "mom", split_axis=0, concat_axis=0, tiled=True))
    other = across(held)
    out = None
    which = core.reshape(1)
    for c in range(CHUNKS):
        out = contract_virtual(k4, which, band_mask, held, other, moved[c], out, c * count, count)
    return out.reshape(2, 64, 1, 2, 8, 256)


def solution(mesh):
    placed = (
        P(None, "mom", None, "band", None, None),
        P("mom", None, None, None),
        P(None, None, "band", None),
        P("mom", None),
        P(),
    )
    return jax.shard_map(
        per_device,
        mesh=mesh,
        in_specs=placed,
        out_specs=P(None, None, "mom", "band", None, None),
        check_vma=False,
    )
```

```python
import jax
import jax.numpy as jnp
from jax import lax
from jax.experimental import pallas as pl
from jax.experimental.pallas import tpu as pltpu
from jax.sharding import PartitionSpec as P

COUNT = 2
PAIR_TYPE = jnp.bfloat16
PIECE = 4
GROUP = 8
MIB = 1 << 20


def wide_rows(coef, wide):
    rows = lax.broadcasted_iota(jnp.int32, (128, 16), 0) // 8
    spread = (rows == lax.broadcasted_iota(jnp.int32, (128, 16), 1)).astype(jnp.bfloat16)
    cols = lax.broadcasted_iota(jnp.int32, (64, 512), 1) // 8
    across = (cols == lax.broadcasted_iota(jnp.int32, (64, 512), 0)).astype(jnp.bfloat16)
    same = lax.broadcasted_iota(jnp.int32, (128, 512), 0) % 8 == lax.broadcasted_iota(jnp.int32, (128, 512), 1) % 8
    tall = jnp.dot(spread, coef, preferred_element_type=jnp.float32).astype(jnp.bfloat16)
    full = jnp.dot(tall, across, preferred_element_type=jnp.float32)
    wide[...] = jnp.where(same, full, 0.0).astype(jnp.bfloat16)


def contract_occupied(coef, ints, first, got=None):
    def kernel(coef_ref, ints_ref, *rest):
        blocks, wide, sems = rest[-3:]
        refs = rest[:-3]

        def copy(c, p):
            return pltpu.make_async_copy(
                ints_ref.at[:, first + c, pl.ds(p * PIECE, PIECE)], blocks.at[c, p], sems.at[c, p]
            )

        for c in range(COUNT):
            for p in range(16 // PIECE):
                copy(c, p).start()
        for c in range(COUNT):
            wide_rows(coef_ref[first + c], wide.at[c])
        for c in range(COUNT):
            for p in range(16 // PIECE):
                copy(c, p).wait()
                for t in range(p * PIECE, p * PIECE + PIECE):
                    sums = jnp.dot(wide[c, :, :256], blocks[c, p, 0, t % PIECE], preferred_element_type=jnp.float32)
                    sums = sums + jnp.dot(
                        wide[c, :, 256:], blocks[c, p, 1, t % PIECE], preferred_element_type=jnp.float32
                    )
                    if got is None:
                        for d in range(4):
                            refs[0][d, t, c] = sums[32 * d : 32 * d + 32].astype(PAIR_TYPE)
                        continue
                    got_ref, own_ref, right_ref, left_ref, up_ref, down_ref = refs
                    total = [sums[32 * d : 32 * d + 32] + got_ref[d, t, c].astype(jnp.float32) for d in range(4)]
                    own_ref[t, c] = total[0]
                    if t < 8:
                        right_ref[t, c] = total[1]
                        up_ref[t, c] = total[2].astype(jnp.bfloat16)
                        down_ref[t, c] = total[3].astype(jnp.bfloat16)
                    else:
                        up_ref[t, c] = total[1].astype(jnp.bfloat16)
                        down_ref[t, c] = total[2].astype(jnp.bfloat16)
                        left_ref[t - 8, c] = total[3]

    vmem = pl.BlockSpec(memory_space=pltpu.VMEM)
    given, shapes = [coef, ints], [jax.ShapeDtypeStruct((4, 16, COUNT, 32, 256), PAIR_TYPE)]
    if got is not None:
        given.append(got)
        shapes = [
            jax.ShapeDtypeStruct((16, COUNT, 32, 256), jnp.float32),
            jax.ShapeDtypeStruct((8, COUNT, 32, 256), jnp.float32),
            jax.ShapeDtypeStruct((8, COUNT, 32, 256), jnp.float32),
            jax.ShapeDtypeStruct((16, COUNT, 32, 256), jnp.bfloat16),
            jax.ShapeDtypeStruct((16, COUNT, 32, 256), jnp.bfloat16),
        ]
    return pl.pallas_call(
        kernel,
        in_specs=[vmem, pl.BlockSpec(memory_space=pltpu.HBM)] + [vmem] * (len(given) - 2),
        out_specs=[vmem] * len(shapes),
        out_shape=shapes,
        scratch_shapes=[
            pltpu.VMEM((COUNT, 16 // PIECE, 2, PIECE, 256, 256), jnp.bfloat16),
            pltpu.VMEM((COUNT, 128, 512), jnp.bfloat16),
            pltpu.SemaphoreType.DMA((COUNT, 16 // PIECE)),
        ],
        compiler_params=pltpu.CompilerParams(vmem_limit_bytes=24 * MIB),
        cost_estimate=pl.CostEstimate(
            flops=COUNT * 16 * 2 * 128 * 512 * 256, bytes_accessed=COUNT * 16 * 300 * 1024, transcendentals=0
        ),
        name="contract_partner" if got is None else "contract_own",
    )(*given)


def code_sums(groups, table):
    def kernel(*refs):
        table_ref, out_ref = refs[-2], refs[-1]
        lane = lax.broadcasted_iota(jnp.int32, (16, 256), 1)
        for t in range(16):
            extra = jnp.zeros((16, 256), jnp.int32)
            for k in range(4):
                own, right, left, up, down = refs[5 * (k // COUNT) : 5 * (k // COUNT) + 5]
                c = k % COUNT
                sums = own[t, c] + (down if t < 8 else up)[t, c].astype(jnp.float32)
                sums = sums + (right[t, c] if t < 8 else left[t - 8, c]).astype(jnp.float32)
                most = jnp.max(jnp.max(jnp.abs(sums), axis=0, keepdims=True), axis=1, keepdims=True)
                power = jnp.floor(jnp.log2(jnp.maximum(most, 1e-30))) + 1.0
                coded = jnp.floor(sums * jnp.exp2(14.5 - power) + 0.5).astype(jnp.int32)
                out_ref[t, 32 * k : 32 * k + 32] = coded.astype(jnp.int16)
                extra = jnp.where(lane == k, table_ref[k, t], extra)
                extra = jnp.where(lane == 4 + k, power.astype(jnp.int32), extra)
            out_ref[t, 128:144] = extra.astype(jnp.int16)

    vmem = pl.BlockSpec(memory_space=pltpu.VMEM)
    given = [x for group in groups for x in group]
    return pl.pallas_call(
        kernel,
        in_specs=[vmem] * len(given) + [pl.BlockSpec(memory_space=pltpu.SMEM)],
        out_specs=vmem,
        out_shape=jax.ShapeDtypeStruct((16, 144, 256), jnp.int16),
        compiler_params=pltpu.CompilerParams(vmem_limit_bytes=24 * MIB),
        name="code_sums",
    )(*given, table)


def contract_virtual(k4, scales, mask, held, u, pair):
    def kernel(k4_ref, scale_ref, mask_ref, held_ref, u_ref, pair_ref, mine_ref, theirs_ref, own, rows, sems):
        def copy(k):
            return pltpu.make_async_copy(held_ref.at[k4_ref[k]], own.at[k], sems.at[k])

        @pl.loop(0, 64)
        def _(k):
            copy(k).start()

        @pl.loop(0, 16)
        def _(j):
            for h, ref in enumerate((u_ref, pair_ref)):
                for c in range(4):
                    full = ref[j, 32 * c : 32 * c + 32].astype(jnp.int32).astype(jnp.float32) * scale_ref[h, 4 * j + c]
                    high = full.astype(jnp.bfloat16)
                    low = (full - high.astype(jnp.float32)).astype(jnp.bfloat16)
                    rows[4 * j + c, 32 * h : 32 * h + 32] = high
                    rows[4 * j + c, 64 + 32 * h : 96 + 32 * h] = low

        @pl.loop(0, 64 // GROUP)
        def _(g):
            for i in range(GROUP):
                copy(g * GROUP + i).wait()
            all_got = []
            for i in range(GROUP):
                k = g * GROUP + i
                both = jnp.concatenate([own[k, 0], own[k, 1]], axis=1)
                all_got.append(jnp.dot(rows[k], both, preferred_element_type=jnp.float32))
            for i in range(GROUP):
                k = g * GROUP + i
                got = all_got[i][:64] + all_got[i][64:]
                keep = mask_ref[pl.ds(k4_ref[k], 1), :]
                for r, ref in ((0, mine_ref), (32, theirs_ref)):
                    ref[0, k] = (got[r : r + 16, :128] - got[r + 16 : r + 32, 128:]) * keep
                    ref[1, k] = (got[r : r + 16, 128:] + got[r + 16 : r + 32, :128]) * keep

    result = jax.ShapeDtypeStruct((2, 64, 16, 128), jnp.float32)
    vmem = pl.BlockSpec(memory_space=pltpu.VMEM)
    return pl.pallas_call(
        kernel,
        in_specs=[pl.BlockSpec(memory_space=pltpu.SMEM)] * 2 + [vmem, pl.BlockSpec(memory_space=pltpu.HBM), vmem, vmem],
        out_specs=[vmem, vmem],
        out_shape=[result, result],
        scratch_shapes=[
            pltpu.VMEM((64, 2, 256, 128), jnp.bfloat16),
            pltpu.VMEM((64, 128, 256), jnp.bfloat16),
            pltpu.SemaphoreType.DMA((64,)),
        ],
        compiler_params=pltpu.CompilerParams(vmem_limit_bytes=24 * MIB),
        cost_estimate=pl.CostEstimate(flops=64 * 2 * 128 * 256 * 256, bytes_accessed=64 * 200 * 1024, transcendentals=0),
        name="contract_virtual",
    )(k4, scales, mask, held, u, pair)


def per_device(ints, vir_coef, occ_coef, k4_table, band_mask):
    mom, band = lax.axis_index("mom"), lax.axis_index("band")
    core, y = band % 2, band // 2

    def across(x):
        return lax.ppermute(x, "band", [(i, i ^ 1) for i in range(8)])

    def along(x, d):
        return lax.ppermute(x, "band", [(i, (i // 2 + d) % 4 * 2 + i % 2) for i in range(8)])

    half = lax.dynamic_slice_in_dim(vir_coef, 128 * core, 128, axis=3)
    held = pltpu.with_memory_space_constraint(lax.all_gather(half, "mom", axis=0, tiled=True), pltpu.HBM)
    mask = lax.dynamic_slice_in_dim(band_mask, 128 * core, 128, axis=1).astype(jnp.float32)

    occ = lax.dynamic_slice_in_dim(occ_coef, 4 * mom, 4, axis=0)
    order = (
        2 * ((core + jnp.arange(2)[:, None, None]) % 2)
        + 4 * ((y + jnp.arange(4)[None, :, None]) % 4)
        + jnp.arange(2)[None, None, :]
    ).reshape(16)
    occ = jnp.take(occ, order, axis=3).reshape(4, 2, 32, 8, 2)
    parts = jnp.stack([jnp.stack([occ[:, 0], -occ[:, 1]], 1), jnp.stack([occ[:, 1], occ[:, 0]], 1)], 1)
    coef = parts.transpose(0, 4, 1, 5, 2, 3).reshape(4, 2, 16, 64)
    coef_own, coef_partner = coef[:, 0], coef[:, 1]

    ints = pltpu.with_memory_space_constraint(ints.reshape(2, 4, 16, 256, 256), pltpu.HBM)
    chunks = range(0, 4, COUNT)
    arrived = [across(contract_occupied(coef_partner, ints, first)[0]) for first in chunks]
    sent = []
    for first, got in zip(chunks, arrived):
        own, right, left, up, down = contract_occupied(coef_own, ints, first, got)
        sent.append((own, right, left, along(up, 1), along(down, -1)))
    groups = []
    for own, right, left, up, down in sent:
        right = along((right + up[:8].astype(jnp.float32)).astype(jnp.bfloat16), 1)
        left = along((left + down[8:].astype(jnp.float32)).astype(jnp.bfloat16), -1)
        groups.append((own, right, left, up, down))
    coded = code_sums(groups, k4_table)
    u = lax.all_to_all(coded, "mom", split_axis=0, concat_axis=0, tiled=True)
    pair = across(u)
    k4 = u[:, 128, :4].astype(jnp.int32).reshape(64)
    powers = jnp.stack([u[:, 128, 4:8], pair[:, 128, 4:8]]).astype(jnp.float32).reshape(2, 64)
    mine, theirs = contract_virtual(k4, jnp.exp2(powers - 14.5), mask, held, u, pair)
    theirs = across(theirs)
    first = jnp.where(core == 0, mine, theirs)
    second = jnp.where(core == 0, theirs, mine)
    return jnp.concatenate([first, second], axis=-1).reshape(2, 64, 1, 2, 8, 256)


def solution(mesh):
    placed = (
        P(None, "mom", None, "band", None, None),
        P("mom", None, None, None),
        P(None, None, "band", None),
        P("mom", None),
        P(),
    )
    return jax.shard_map(
        per_device,
        mesh=mesh,
        in_specs=placed,
        out_specs=P(None, None, "mom", "band", None, None),
        check_vma=False,
    )
```

```python
import jax
import jax.numpy as jnp
from jax import lax
from jax.experimental import pallas as pl
from jax.experimental.pallas import tpu as pltpu
from jax.sharding import PartitionSpec as P

COUNT = 2
PAIR_TYPE = jnp.bfloat16
PIECE = 4
MIB = 1 << 20
LIGHT = pl.CostEstimate(flops=1, bytes_accessed=1, transcendentals=0)


def wide_rows(coef, wide):
    rows = lax.broadcasted_iota(jnp.int32, (128, 16), 0) // 8
    spread = (rows == lax.broadcasted_iota(jnp.int32, (128, 16), 1)).astype(jnp.bfloat16)
    cols = lax.broadcasted_iota(jnp.int32, (64, 512), 1) // 8
    across = (cols == lax.broadcasted_iota(jnp.int32, (64, 512), 0)).astype(jnp.bfloat16)
    same = lax.broadcasted_iota(jnp.int32, (128, 512), 0) % 8 == lax.broadcasted_iota(jnp.int32, (128, 512), 1) % 8
    tall = jnp.dot(spread, coef, preferred_element_type=jnp.float32).astype(jnp.bfloat16)
    full = jnp.dot(tall, across, preferred_element_type=jnp.float32)
    wide[...] = jnp.where(same, full, 0.0).astype(jnp.bfloat16)


def contract_occupied(coef, ints, first, got=None):
    def kernel(coef_ref, ints_ref, *rest):
        blocks, wide, sems = rest[-3:]
        refs = rest[:-3]

        def copy(c, p):
            return pltpu.make_async_copy(
                ints_ref.at[:, first + c, pl.ds(p * PIECE, PIECE)], blocks.at[c, p], sems.at[c, p]
            )

        for c in range(COUNT):
            for p in range(16 // PIECE):
                copy(c, p).start()
        for c in range(COUNT):
            wide_rows(coef_ref[first + c], wide.at[c])
        for c in range(COUNT):
            for p in range(16 // PIECE):
                copy(c, p).wait()
                for t in range(p * PIECE, p * PIECE + PIECE):
                    sums = jnp.dot(wide[c, :, :256], blocks[c, p, 0, t % PIECE], preferred_element_type=jnp.float32)
                    sums = sums + jnp.dot(
                        wide[c, :, 256:], blocks[c, p, 1, t % PIECE], preferred_element_type=jnp.float32
                    )
                    if got is None:
                        for d in range(4):
                            refs[0][d, t, c] = sums[32 * d : 32 * d + 32].astype(PAIR_TYPE)
                        continue
                    got_ref, own_ref, right_ref, left_ref, up_ref, down_ref = refs
                    total = [sums[32 * d : 32 * d + 32] + got_ref[d, t, c].astype(jnp.float32) for d in range(4)]
                    own_ref[t, c] = total[0]
                    if t < 8:
                        right_ref[t, c] = total[1]
                        up_ref[t, c] = total[2].astype(jnp.bfloat16)
                        down_ref[t, c] = total[3].astype(jnp.bfloat16)
                    else:
                        up_ref[t, c] = total[1].astype(jnp.bfloat16)
                        down_ref[t, c] = total[2].astype(jnp.bfloat16)
                        left_ref[t - 8, c] = total[3]

    vmem = pl.BlockSpec(memory_space=pltpu.VMEM)
    given, shapes = [coef, ints], [jax.ShapeDtypeStruct((4, 16, COUNT, 32, 256), PAIR_TYPE)]
    if got is not None:
        given.append(got)
        shapes = [
            jax.ShapeDtypeStruct((16, COUNT, 32, 256), jnp.float32),
            jax.ShapeDtypeStruct((8, COUNT, 32, 256), jnp.float32),
            jax.ShapeDtypeStruct((8, COUNT, 32, 256), jnp.float32),
            jax.ShapeDtypeStruct((16, COUNT, 32, 256), jnp.bfloat16),
            jax.ShapeDtypeStruct((16, COUNT, 32, 256), jnp.bfloat16),
        ]
    return pl.pallas_call(
        kernel,
        in_specs=[vmem, pl.BlockSpec(memory_space=pltpu.HBM)] + [vmem] * (len(given) - 2),
        out_specs=[vmem] * len(shapes),
        out_shape=shapes,
        scratch_shapes=[
            pltpu.VMEM((COUNT, 16 // PIECE, 2, PIECE, 256, 256), jnp.bfloat16),
            pltpu.VMEM((COUNT, 128, 512), jnp.bfloat16),
            pltpu.SemaphoreType.DMA((COUNT, 16 // PIECE)),
        ],
        compiler_params=pltpu.CompilerParams(vmem_limit_bytes=18 * MIB),
        cost_estimate=LIGHT,
        name="contract_partner" if got is None else "contract_own",
    )(*given)


def code_sums(owns, ups, downs, right, left, table):
    n = len(owns)

    def kernel(*refs):
        own_refs, up_refs, down_refs = refs[:n], refs[n : 2 * n], refs[2 * n : 3 * n]
        right_ref, left_ref, table_ref, out_ref = refs[3 * n :]
        line = lax.broadcasted_iota(jnp.int32, (16, 256), 0)
        lane = lax.broadcasted_iota(jnp.int32, (16, 256), 1)
        for t in range(16):
            extra = jnp.zeros((16, 256), jnp.int32)
            for k in range(4):
                i, c = k // COUNT, k % COUNT
                sums = own_refs[i][t, c] + (down_refs if t < 8 else up_refs)[i][t, c].astype(jnp.float32)
                sums = sums + (right_ref[t, k] if t < 8 else left_ref[t - 8, k]).astype(jnp.float32)
                most = jnp.max(jnp.max(jnp.abs(sums), axis=0, keepdims=True), axis=1, keepdims=True)
                power = jnp.floor(jnp.log2(jnp.maximum(most, 1e-30))) + 1.0
                coded = jnp.floor(sums * jnp.exp2(14.5 - power) + 0.5).astype(jnp.int32)
                out_ref[t, 32 * k : 32 * k + 32] = coded.astype(jnp.int16)
                extra = jnp.where((line == 0) & (lane == k), table_ref[k, t], extra)
                extra = jnp.where(line == 1 + k, power.astype(jnp.int32), extra)
            out_ref[t, 128:144] = extra.astype(jnp.int16)

    vmem = pl.BlockSpec(memory_space=pltpu.VMEM)
    return pl.pallas_call(
        kernel,
        in_specs=[vmem] * (3 * n + 2) + [pl.BlockSpec(memory_space=pltpu.SMEM)],
        out_specs=vmem,
        out_shape=jax.ShapeDtypeStruct((16, 144, 256), jnp.int16),
        compiler_params=pltpu.CompilerParams(vmem_limit_bytes=18 * MIB),
        cost_estimate=LIGHT,
        name="code_sums",
    )(*owns, *ups, *downs, right, left, table)


def contract_virtual(k4, k2, mask, held, u, pair):
    sizes = [x.shape[0] for x in held]
    starts = [sum(sizes[:i]) for i in range(len(held))]

    def kernel(k4_ref, k2_ref, mask_ref, u_ref, pair_ref, *rest):
        held_refs, (mine_ref, theirs_ref, blocks, rows, sems) = rest[: len(held)], rest[len(held) :]

        def copy(i):
            return pltpu.make_async_copy(held_refs[i], blocks.at[pl.ds(starts[i], sizes[i])], sems.at[i])

        for i in range(len(held)):
            copy(i).start()

        @pl.loop(0, 16)
        def _(j):
            for h, ref in enumerate((u_ref, pair_ref)):
                scale = jnp.exp2(ref[j, 128:144].astype(jnp.int32).astype(jnp.float32) - 14.5)
                for c in range(4):
                    full = ref[j, 32 * c : 32 * c + 32].astype(jnp.int32).astype(jnp.float32) * scale[1 + c : 2 + c]
                    high = full.astype(jnp.bfloat16)
                    low = (full - high.astype(jnp.float32)).astype(jnp.bfloat16)
                    rows[4 * j + c, 32 * h : 32 * h + 32] = high
                    rows[4 * j + c, 64 + 32 * h : 96 + 32 * h] = low

        for first in range(0, 64, 8):
            if first in starts:
                copy(starts.index(first)).wait()
            all_got = []
            for n in range(first, first + 8):
                both = jnp.concatenate([blocks[n, 0], blocks[n, 1]], axis=1)
                all_got.append(jnp.dot(rows[k2_ref[n]], both, preferred_element_type=jnp.float32))
            for n in range(first, first + 8):
                k = k2_ref[n]
                got = all_got[n - first][:64] + all_got[n - first][64:]
                keep = mask_ref[pl.ds(k4_ref[n], 1), :]
                for r, ref in ((0, mine_ref), (32, theirs_ref)):
                    ref[0, k] = (got[r : r + 16, :128] - got[r + 16 : r + 32, 128:]) * keep
                    ref[1, k] = (got[r : r + 16, 128:] + got[r + 16 : r + 32, :128]) * keep

    result = jax.ShapeDtypeStruct((2, 64, 16, 128), jnp.float32)
    vmem = pl.BlockSpec(memory_space=pltpu.VMEM)
    return pl.pallas_call(
        kernel,
        in_specs=[pl.BlockSpec(memory_space=pltpu.SMEM)] * 2
        + [vmem] * 3
        + [pl.BlockSpec(memory_space=pltpu.HBM)] * len(held),
        out_specs=[vmem, vmem],
        out_shape=[result, result],
        scratch_shapes=[
            pltpu.VMEM((64, 2, 256, 128), jnp.bfloat16),
            pltpu.VMEM((64, 128, 256), jnp.bfloat16),
            pltpu.SemaphoreType.DMA((len(held),)),
        ],
        compiler_params=pltpu.CompilerParams(vmem_limit_bytes=18 * MIB),
        cost_estimate=LIGHT,
        name="contract_virtual",
    )(k4, k2, mask, u, pair, *held)


def per_device(ints, vir_coef, occ_coef, k4_table, band_mask):
    mom, band = lax.axis_index("mom"), lax.axis_index("band")
    core, y = band % 2, band // 2

    def across(x):
        return lax.ppermute(x, "band", [(i, i ^ 1) for i in range(8)])

    def along(x, d):
        return lax.ppermute(x, "band", [(i, (i // 2 + d) % 4 * 2 + i % 2) for i in range(8)])

    half = lax.dynamic_slice_in_dim(vir_coef, 128 * core, 128, axis=3)

    def onward(v, second, d):
        pairs = []
        for i in range(16):
            for j in range(8):
                to = (i // 4 + d) % 4 * 4 + i % 4 if (j % 2 == 1) != second else i // 4 * 4 + (i % 4 + d) % 4
                pairs.append((8 * i + j, 8 * to + j))
        return lax.ppermute(v, ("mom", "band"), pairs)

    offset = jnp.array([0, -1, 1, 2])
    n = jnp.arange(64)
    within, beyond, local = offset[n // 4 % 4], offset[n // 16], n % 4
    x = mom // 4 + jnp.where(core == 0, beyond, within)
    z = mom % 4 + jnp.where(core == 0, within, beyond)
    held_k4 = 4 * (4 * (x % 4) + z % 4) + local
    mask = lax.dynamic_slice_in_dim(band_mask, 128 * core, 128, axis=1).astype(jnp.float32)

    occ = lax.dynamic_slice_in_dim(occ_coef, 4 * mom, 4, axis=0)
    order = (
        2 * ((core + jnp.arange(2)[:, None, None]) % 2)
        + 4 * ((y + jnp.arange(4)[None, :, None]) % 4)
        + jnp.arange(2)[None, None, :]
    ).reshape(16)
    occ = jnp.take(occ, order, axis=3).reshape(4, 2, 32, 8, 2)
    parts = jnp.stack([jnp.stack([occ[:, 0], -occ[:, 1]], 1), jnp.stack([occ[:, 1], occ[:, 0]], 1)], 1)
    coef = parts.transpose(0, 4, 1, 5, 2, 3).reshape(4, 2, 16, 64)
    coef_own, coef_partner = coef[:, 0], coef[:, 1]

    ints = pltpu.with_memory_space_constraint(ints.reshape(2, 4, 16, 256, 256), pltpu.HBM)
    def after(x, *others):
        return lax.optimization_barrier((x, *others))[0]

    theirs = contract_occupied(coef_partner, ints, 0)[0]
    got = across(theirs)
    half = after(half, theirs)
    near = [onward(half, False, d) for d in (1, -1, 2)]
    own, right, left, up, down = contract_occupied(coef_own, ints, 0, got)
    ups, downs = [along(up, 1)], [along(down, -1)]
    owns, rights, lefts = [own], [right], [left]
    near = lax.optimization_barrier((*near, up))[:3]
    row = jnp.concatenate([half, *near])
    below, above = onward(row, True, 1), onward(row, True, -1)
    got = across(contract_occupied(after(coef_partner, up), ints, COUNT)[0])
    own, right, left, up, down = contract_occupied(coef_own, ints, COUNT, got)
    ups.append(along(up, 1))
    downs.append(along(down, -1))
    owns, rights, lefts = owns + [own], rights + [right], lefts + [left]
    right = [(r + x[:8].astype(jnp.float32)).astype(jnp.bfloat16) for r, x in zip(rights, ups)]
    left = [(r + x[8:].astype(jnp.float32)).astype(jnp.bfloat16) for r, x in zip(lefts, downs)]
    right, left = jnp.concatenate(right, axis=1), jnp.concatenate(left, axis=1)
    low, high = lax.optimization_barrier((below[:8], above[8:], up, down))[:2]
    opposite = [onward(low, True, 1), onward(high, True, -1)]
    held = [row, below, above] + opposite
    owns[0] = after(owns[0], *opposite)
    coded = code_sums(owns, ups, downs, along(right, 1), along(left, -1), k4_table)
    u = lax.all_to_all(coded, "mom", split_axis=0, concat_axis=0, tiled=True)
    pair = across(u)
    k4 = u[:, 128, :4].astype(jnp.int32).reshape(64)
    k2 = jnp.sum(jnp.where(held_k4[:, None] == k4[None, :], n[None, :], 0), axis=1)
    held = [pltpu.with_memory_space_constraint(x, pltpu.HBM) for x in held]
    mine, theirs = contract_virtual(held_k4, k2, mask, held, u, pair)
    theirs = across(theirs)
    low, high = jnp.concatenate([mine, theirs], axis=-1), jnp.concatenate([theirs, mine], axis=-1)
    return jnp.where(core == 0, low, high).reshape(2, 64, 1, 2, 8, 256)


def solution(mesh):
    placed = (
        P(None, "mom", None, "band", None, None),
        P("mom", None, None, None),
        P(None, None, "band", None),
        P("mom", None),
        P(),
    )
    return jax.shard_map(
        per_device,
        mesh=mesh,
        in_specs=placed,
        out_specs=P(None, None, "mom", "band", None, None),
        check_vma=False,
    )
```

```python
import jax
import jax.numpy as jnp
from jax import lax
from jax.experimental import pallas as pl
from jax.experimental.pallas import tpu as pltpu
from jax.sharding import PartitionSpec as P

COUNT = 2
PAIR_TYPE = jnp.bfloat16
PIECE = 4
MIB = 1 << 20
LIGHT = pl.CostEstimate(flops=1, bytes_accessed=1, transcendentals=0)


def wide_rows(coef, wide):
    rows = lax.broadcasted_iota(jnp.int32, (128, 16), 0) // 8
    spread = (rows == lax.broadcasted_iota(jnp.int32, (128, 16), 1)).astype(jnp.bfloat16)
    cols = lax.broadcasted_iota(jnp.int32, (64, 512), 1) // 8
    across = (cols == lax.broadcasted_iota(jnp.int32, (64, 512), 0)).astype(jnp.bfloat16)
    same = lax.broadcasted_iota(jnp.int32, (128, 512), 0) % 8 == lax.broadcasted_iota(jnp.int32, (128, 512), 1) % 8
    tall = jnp.dot(spread, coef, preferred_element_type=jnp.float32).astype(jnp.bfloat16)
    full = jnp.dot(tall, across, preferred_element_type=jnp.float32)
    wide[...] = jnp.where(same, full, 0.0).astype(jnp.bfloat16)


def contract_occupied(coef, ints, first, got=None):
    def kernel(coef_ref, ints_ref, *rest):
        blocks, wide, sems = rest[-3:]
        refs = rest[:-3]

        def copy(c, p):
            return pltpu.make_async_copy(
                ints_ref.at[:, first + c, pl.ds(p * PIECE, PIECE)], blocks.at[c, p], sems.at[c, p]
            )

        for c in range(COUNT):
            for p in range(16 // PIECE):
                copy(c, p).start()
        for c in range(COUNT):
            wide_rows(coef_ref[first + c], wide.at[c])
        for c in range(COUNT):
            for p in range(16 // PIECE):
                copy(c, p).wait()
                for t in range(p * PIECE, p * PIECE + PIECE):
                    sums = jnp.dot(wide[c, :, :256], blocks[c, p, 0, t % PIECE], preferred_element_type=jnp.float32)
                    sums = sums + jnp.dot(
                        wide[c, :, 256:], blocks[c, p, 1, t % PIECE], preferred_element_type=jnp.float32
                    )
                    if got is None:
                        for d in range(4):
                            refs[0][d, t, c] = sums[32 * d : 32 * d + 32].astype(PAIR_TYPE)
                        continue
                    got_ref, own_ref, right_ref, left_ref, up_ref, down_ref = refs
                    total = [sums[32 * d : 32 * d + 32] + got_ref[d, t, c].astype(jnp.float32) for d in range(4)]
                    own_ref[t, c] = total[0]
                    if t < 8:
                        right_ref[t, c] = total[1]
                        up_ref[t, c] = total[2].astype(jnp.bfloat16)
                        down_ref[t, c] = total[3].astype(jnp.bfloat16)
                    else:
                        up_ref[t, c] = total[1].astype(jnp.bfloat16)
                        down_ref[t, c] = total[2].astype(jnp.bfloat16)
                        left_ref[t - 8, c] = total[3]

    vmem = pl.BlockSpec(memory_space=pltpu.VMEM)
    given, shapes = [coef, ints], [jax.ShapeDtypeStruct((4, 16, COUNT, 32, 256), PAIR_TYPE)]
    if got is not None:
        given.append(got)
        shapes = [
            jax.ShapeDtypeStruct((16, COUNT, 32, 256), jnp.float32),
            jax.ShapeDtypeStruct((8, COUNT, 32, 256), jnp.float32),
            jax.ShapeDtypeStruct((8, COUNT, 32, 256), jnp.float32),
            jax.ShapeDtypeStruct((16, COUNT, 32, 256), jnp.bfloat16),
            jax.ShapeDtypeStruct((16, COUNT, 32, 256), jnp.bfloat16),
        ]
    return pl.pallas_call(
        kernel,
        in_specs=[vmem, pl.BlockSpec(memory_space=pltpu.HBM)] + [vmem] * (len(given) - 2),
        out_specs=[vmem] * len(shapes),
        out_shape=shapes,
        scratch_shapes=[
            pltpu.VMEM((COUNT, 16 // PIECE, 2, PIECE, 256, 256), jnp.bfloat16),
            pltpu.VMEM((COUNT, 128, 512), jnp.bfloat16),
            pltpu.SemaphoreType.DMA((COUNT, 16 // PIECE)),
        ],
        compiler_params=pltpu.CompilerParams(vmem_limit_bytes=18 * MIB),
        cost_estimate=LIGHT,
        name="contract_partner" if got is None else "contract_own",
    )(*given)


def code_sums(owns, ups, downs, right, left, table):
    n = len(owns)

    def kernel(*refs):
        own_refs, up_refs, down_refs = refs[:n], refs[n : 2 * n], refs[2 * n : 3 * n]
        right_ref, left_ref, table_ref, out_ref = refs[3 * n :]
        line = lax.broadcasted_iota(jnp.int32, (16, 256), 0)
        lane = lax.broadcasted_iota(jnp.int32, (16, 256), 1)
        for t in range(16):
            extra = jnp.zeros((16, 256), jnp.int32)
            for k in range(4):
                i, c = k // COUNT, k % COUNT
                sums = own_refs[i][t, c] + (down_refs if t < 8 else up_refs)[i][t, c].astype(jnp.float32)
                sums = sums + (right_ref[t, k] if t < 8 else left_ref[t - 8, k]).astype(jnp.float32)
                most = jnp.max(jnp.max(jnp.abs(sums), axis=0, keepdims=True), axis=1, keepdims=True)
                power = jnp.floor(jnp.log2(jnp.maximum(most, 1e-30))) + 1.0
                coded = jnp.floor(sums * jnp.exp2(14.5 - power) + 0.5).astype(jnp.int32)
                out_ref[t, 32 * k : 32 * k + 32] = coded.astype(jnp.int16)
                extra = jnp.where((line == 0) & (lane == k), table_ref[k, t], extra)
                extra = jnp.where(line == 1 + k, power.astype(jnp.int32), extra)
            out_ref[t, 128:144] = extra.astype(jnp.int16)

    vmem = pl.BlockSpec(memory_space=pltpu.VMEM)
    return pl.pallas_call(
        kernel,
        in_specs=[vmem] * (3 * n + 2) + [pl.BlockSpec(memory_space=pltpu.SMEM)],
        out_specs=vmem,
        out_shape=jax.ShapeDtypeStruct((16, 144, 256), jnp.int16),
        compiler_params=pltpu.CompilerParams(vmem_limit_bytes=18 * MIB),
        cost_estimate=LIGHT,
        name="code_sums",
    )(*owns, *ups, *downs, right, left, table)


def contract_virtual(k4, k2, mask, held, u, pair):
    sizes = [x.shape[0] for x in held]
    starts = [sum(sizes[:i]) for i in range(len(held))]

    def kernel(k4_ref, k2_ref, mask_ref, u_ref, pair_ref, *rest):
        held_refs, (mine_ref, theirs_ref, blocks, rows, sems) = rest[: len(held)], rest[len(held) :]

        def copy(i):
            return pltpu.make_async_copy(held_refs[i], blocks.at[pl.ds(starts[i], sizes[i])], sems.at[i])

        for i in range(len(held)):
            copy(i).start()

        @pl.loop(0, 16)
        def _(j):
            for h, ref in enumerate((u_ref, pair_ref)):
                scale = jnp.exp2(ref[j, 128:144].astype(jnp.int32).astype(jnp.float32) - 14.5)
                for c in range(4):
                    full = ref[j, 32 * c : 32 * c + 32].astype(jnp.int32).astype(jnp.float32) * scale[1 + c : 2 + c]
                    high = full.astype(jnp.bfloat16)
                    low = (full - high.astype(jnp.float32)).astype(jnp.bfloat16)
                    rows[4 * j + c, 32 * h : 32 * h + 32] = high
                    rows[4 * j + c, 64 + 32 * h : 96 + 32 * h] = low

        for first in range(0, 64, 8):
            if first in starts:
                copy(starts.index(first)).wait()
            all_got = []
            for n in range(first, first + 8):
                both = jnp.concatenate([blocks[n, 0], blocks[n, 1]], axis=1)
                all_got.append(jnp.dot(rows[k2_ref[n]], both, preferred_element_type=jnp.float32))
            for n in range(first, first + 8):
                k = k2_ref[n]
                got = all_got[n - first][:64] + all_got[n - first][64:]
                keep = mask_ref[pl.ds(k4_ref[n], 1), :]
                for r, ref in ((0, mine_ref), (32, theirs_ref)):
                    ref[0, k] = (got[r : r + 16, :128] - got[r + 16 : r + 32, 128:]) * keep
                    ref[1, k] = (got[r : r + 16, 128:] + got[r + 16 : r + 32, :128]) * keep

    result = jax.ShapeDtypeStruct((2, 64, 16, 128), jnp.float32)
    vmem = pl.BlockSpec(memory_space=pltpu.VMEM)
    return pl.pallas_call(
        kernel,
        in_specs=[pl.BlockSpec(memory_space=pltpu.SMEM)] * 2
        + [vmem] * 3
        + [pl.BlockSpec(memory_space=pltpu.HBM)] * len(held),
        out_specs=[vmem, vmem],
        out_shape=[result, result],
        scratch_shapes=[
            pltpu.VMEM((64, 2, 256, 128), jnp.bfloat16),
            pltpu.VMEM((64, 128, 256), jnp.bfloat16),
            pltpu.SemaphoreType.DMA((len(held),)),
        ],
        compiler_params=pltpu.CompilerParams(vmem_limit_bytes=18 * MIB),
        cost_estimate=LIGHT,
        name="contract_virtual",
    )(k4, k2, mask, u, pair, *held)


def per_device(ints, vir_coef, occ_coef, k4_table, band_mask):
    mom, band = lax.axis_index("mom"), lax.axis_index("band")
    core, y = band % 2, band // 2

    def across(x):
        return lax.ppermute(x, "band", [(i, i ^ 1) for i in range(8)])

    def along(x, d):
        return lax.ppermute(x, "band", [(i, (i // 2 + d) % 4 * 2 + i % 2) for i in range(8)])

    half = lax.dynamic_slice_in_dim(vir_coef, 128 * core, 128, axis=3)

    def onward(v, second, d):
        pairs = []
        for i in range(16):
            for j in range(8):
                to = (i // 4 + d) % 4 * 4 + i % 4 if (j % 2 == 1) != second else i // 4 * 4 + (i % 4 + d) % 4
                pairs.append((8 * i + j, 8 * to + j))
        return lax.ppermute(v, ("mom", "band"), pairs)

    offset = jnp.array([0, -1, 1, 2])
    n = jnp.arange(64)
    within, beyond, local = offset[n // 4 % 4], offset[n // 16], n % 4
    x = mom // 4 + jnp.where(core == 0, beyond, within)
    z = mom % 4 + jnp.where(core == 0, within, beyond)
    held_k4 = 4 * (4 * (x % 4) + z % 4) + local
    mask = lax.dynamic_slice_in_dim(band_mask, 128 * core, 128, axis=1).astype(jnp.float32)

    occ = lax.dynamic_slice_in_dim(occ_coef, 4 * mom, 4, axis=0)
    order = (
        2 * ((core + jnp.arange(2)[:, None, None]) % 2)
        + 4 * ((y + jnp.arange(4)[None, :, None]) % 4)
        + jnp.arange(2)[None, None, :]
    ).reshape(16)
    occ = jnp.take(occ, order, axis=3).reshape(4, 2, 32, 8, 2)
    parts = jnp.stack([jnp.stack([occ[:, 0], -occ[:, 1]], 1), jnp.stack([occ[:, 1], occ[:, 0]], 1)], 1)
    coef = parts.transpose(0, 4, 1, 5, 2, 3).reshape(4, 2, 16, 64)
    coef_own, coef_partner = coef[:, 0], coef[:, 1]

    ints = pltpu.with_memory_space_constraint(ints.reshape(2, 4, 16, 256, 256), pltpu.HBM)
    def after(x, *others):
        return lax.optimization_barrier((x, *others))[0]

    near = [onward(half, False, d) for d in (1, -1, 2)]
    row = jnp.concatenate([half, *near])
    below, above = onward(row, True, 1), onward(row, True, -1)
    chunks = range(0, 4, COUNT)
    partner = [contract_occupied(coef_partner, ints, first)[0] for first in chunks]
    arrived = [across(x) for x in partner]
    arrived[0] = after(arrived[0], row)
    sent = [contract_occupied(coef_own, ints, first, got) for first, got in zip(chunks, arrived)]
    owns, rights, lefts = [x[0] for x in sent], [x[1] for x in sent], [x[2] for x in sent]
    ups, downs = [along(x[3], 1) for x in sent], [along(x[4], -1) for x in sent]
    right = [(r + x[:8].astype(jnp.float32)).astype(jnp.bfloat16) for r, x in zip(rights, ups)]
    left = [(r + x[8:].astype(jnp.float32)).astype(jnp.bfloat16) for r, x in zip(lefts, downs)]
    right, left = jnp.concatenate(right, axis=1), jnp.concatenate(left, axis=1)
    low, high = lax.optimization_barrier((below[:8], above[8:], left))[:2]
    opposite = [onward(low, True, 1), onward(high, True, -1)]
    held = [row, below, above] + opposite
    owns[0] = after(owns[0], *opposite)
    coded = code_sums(owns, ups, downs, along(right, 1), along(left, -1), k4_table)
    u = lax.all_to_all(coded, "mom", split_axis=0, concat_axis=0, tiled=True)
    pair = across(u)
    k4 = u[:, 128, :4].astype(jnp.int32).reshape(64)
    k2 = jnp.sum(jnp.where(held_k4[:, None] == k4[None, :], n[None, :], 0), axis=1)
    held = [pltpu.with_memory_space_constraint(x, pltpu.HBM) for x in held]
    mine, theirs = contract_virtual(held_k4, k2, mask, held, u, pair)
    theirs = across(theirs)
    low, high = jnp.concatenate([mine, theirs], axis=-1), jnp.concatenate([theirs, mine], axis=-1)
    return jnp.where(core == 0, low, high).reshape(2, 64, 1, 2, 8, 256)


def solution(mesh):
    placed = (
        P(None, "mom", None, "band", None, None),
        P("mom", None, None, None),
        P(None, None, "band", None),
        P("mom", None),
        P(),
    )
    return jax.shard_map(
        per_device,
        mesh=mesh,
        in_specs=placed,
        out_specs=P(None, None, "mom", "band", None, None),
        check_vma=False,
    )
```

```python
import jax
import jax.numpy as jnp
from jax import lax
from jax.experimental import pallas as pl
from jax.experimental.pallas import tpu as pltpu
from jax.sharding import PartitionSpec as P

COUNT = 2
PAIR_TYPE = jnp.bfloat16
PIECE = 4
MIB = 1 << 20
LIGHT = pl.CostEstimate(flops=1, bytes_accessed=1, transcendentals=0)


def wide_rows(coef, wide):
    rows = lax.broadcasted_iota(jnp.int32, (128, 16), 0) // 8
    spread = (rows == lax.broadcasted_iota(jnp.int32, (128, 16), 1)).astype(jnp.bfloat16)
    cols = lax.broadcasted_iota(jnp.int32, (64, 512), 1) // 8
    across = (cols == lax.broadcasted_iota(jnp.int32, (64, 512), 0)).astype(jnp.bfloat16)
    same = lax.broadcasted_iota(jnp.int32, (128, 512), 0) % 8 == lax.broadcasted_iota(jnp.int32, (128, 512), 1) % 8
    tall = jnp.dot(spread, coef, preferred_element_type=jnp.float32).astype(jnp.bfloat16)
    full = jnp.dot(tall, across, preferred_element_type=jnp.float32)
    wide[...] = jnp.where(same, full, 0.0).astype(jnp.bfloat16)


def contract_occupied(coef, ints, first, got=None):
    def kernel(coef_ref, ints_ref, *rest):
        blocks, wide, sems = rest[-3:]
        refs = rest[:-3]

        def copy(c, p):
            return pltpu.make_async_copy(
                ints_ref.at[:, first + c, pl.ds(p * PIECE, PIECE)], blocks.at[c, p], sems.at[c, p]
            )

        for c in range(COUNT):
            for p in range(16 // PIECE):
                copy(c, p).start()
        for c in range(COUNT):
            wide_rows(coef_ref[first + c], wide.at[c])
        for c in range(COUNT):
            for p in range(16 // PIECE):
                copy(c, p).wait()
                for t in range(p * PIECE, p * PIECE + PIECE):
                    sums = jnp.dot(wide[c, :, :256], blocks[c, p, 0, t % PIECE], preferred_element_type=jnp.float32)
                    sums = sums + jnp.dot(
                        wide[c, :, 256:], blocks[c, p, 1, t % PIECE], preferred_element_type=jnp.float32
                    )
                    if got is None:
                        for d in range(4):
                            refs[0][d, t, c] = sums[32 * d : 32 * d + 32].astype(PAIR_TYPE)
                        continue
                    got_ref, own_ref, right_ref, left_ref, up_ref, down_ref = refs
                    total = [sums[32 * d : 32 * d + 32] + got_ref[d, t, c].astype(jnp.float32) for d in range(4)]
                    own_ref[t, c] = total[0]
                    if t < 8:
                        right_ref[t, c] = total[1]
                        up_ref[t, c] = total[2].astype(jnp.bfloat16)
                        down_ref[t, c] = total[3].astype(jnp.bfloat16)
                    else:
                        up_ref[t, c] = total[1].astype(jnp.bfloat16)
                        down_ref[t, c] = total[2].astype(jnp.bfloat16)
                        left_ref[t - 8, c] = total[3]

    vmem = pl.BlockSpec(memory_space=pltpu.VMEM)
    given, shapes = [coef, ints], [jax.ShapeDtypeStruct((4, 16, COUNT, 32, 256), PAIR_TYPE)]
    if got is not None:
        given.append(got)
        shapes = [
            jax.ShapeDtypeStruct((16, COUNT, 32, 256), jnp.float32),
            jax.ShapeDtypeStruct((8, COUNT, 32, 256), jnp.float32),
            jax.ShapeDtypeStruct((8, COUNT, 32, 256), jnp.float32),
            jax.ShapeDtypeStruct((16, COUNT, 32, 256), jnp.bfloat16),
            jax.ShapeDtypeStruct((16, COUNT, 32, 256), jnp.bfloat16),
        ]
    return pl.pallas_call(
        kernel,
        in_specs=[vmem, pl.BlockSpec(memory_space=pltpu.HBM)] + [vmem] * (len(given) - 2),
        out_specs=[vmem] * len(shapes),
        out_shape=shapes,
        scratch_shapes=[
            pltpu.VMEM((COUNT, 16 // PIECE, 2, PIECE, 256, 256), jnp.bfloat16),
            pltpu.VMEM((COUNT, 128, 512), jnp.bfloat16),
            pltpu.SemaphoreType.DMA((COUNT, 16 // PIECE)),
        ],
        compiler_params=pltpu.CompilerParams(vmem_limit_bytes=18 * MIB),
        cost_estimate=LIGHT,
        name="contract_partner" if got is None else "contract_own",
    )(*given)


def code_sums(owns, ups, downs, right, left, table):
    n = len(owns)

    def kernel(*refs):
        own_refs, down_refs = refs[:n], refs[n : 2 * n]
        up_ref, right_ref, left_ref, table_ref, out_ref = refs[2 * n :]
        line = lax.broadcasted_iota(jnp.int32, (16, 256), 0)
        lane = lax.broadcasted_iota(jnp.int32, (16, 256), 1)
        for t in range(16):
            extra = jnp.zeros((16, 256), jnp.int32)
            for k in range(4):
                i, c = k // COUNT, k % COUNT
                sums = own_refs[i][t, c] + (down_refs[i][t, c] if t < 8 else up_ref[t, k]).astype(jnp.float32)
                sums = sums + (right_ref[t, k] if t < 8 else left_ref[t - 8, k]).astype(jnp.float32)
                most = jnp.max(jnp.max(jnp.abs(sums), axis=0, keepdims=True), axis=1, keepdims=True)
                power = jnp.floor(jnp.log2(jnp.maximum(most, 1e-30))) + 1.0
                coded = jnp.floor(sums * jnp.exp2(14.5 - power) + 0.5).astype(jnp.int32)
                out_ref[t, 32 * k : 32 * k + 32] = coded.astype(jnp.int16)
                extra = jnp.where((line == 0) & (lane == k), table_ref[k, t], extra)
                extra = jnp.where(line == 1 + k, power.astype(jnp.int32), extra)
            out_ref[t, 128:144] = extra.astype(jnp.int16)

    vmem = pl.BlockSpec(memory_space=pltpu.VMEM)
    return pl.pallas_call(
        kernel,
        in_specs=[vmem] * (2 * n + 3) + [pl.BlockSpec(memory_space=pltpu.SMEM)],
        out_specs=vmem,
        out_shape=jax.ShapeDtypeStruct((16, 144, 256), jnp.int16),
        compiler_params=pltpu.CompilerParams(vmem_limit_bytes=18 * MIB),
        cost_estimate=LIGHT,
        name="code_sums",
    )(*owns, *downs, ups, right, left, table)


def contract_virtual(k4, k2, mask, held, u, pair):
    sizes = [x.shape[0] for x in held]
    starts = [sum(sizes[:i]) for i in range(len(held))]

    def kernel(k4_ref, k2_ref, mask_ref, u_ref, pair_ref, *rest):
        held_refs, (mine_ref, theirs_ref, blocks, rows, sems) = rest[: len(held)], rest[len(held) :]

        def copy(i):
            return pltpu.make_async_copy(held_refs[i], blocks.at[pl.ds(starts[i], sizes[i])], sems.at[i])

        for i in range(len(held)):
            copy(i).start()

        @pl.loop(0, 16)
        def _(j):
            for h, ref in enumerate((u_ref, pair_ref)):
                scale = jnp.exp2(ref[j, 128:144].astype(jnp.int32).astype(jnp.float32) - 14.5)
                for c in range(4):
                    full = ref[j, 32 * c : 32 * c + 32].astype(jnp.int32).astype(jnp.float32) * scale[1 + c : 2 + c]
                    high = full.astype(jnp.bfloat16)
                    low = (full - high.astype(jnp.float32)).astype(jnp.bfloat16)
                    rows[4 * j + c, 32 * h : 32 * h + 32] = high
                    rows[4 * j + c, 64 + 32 * h : 96 + 32 * h] = low

        for first in range(0, 64, 8):
            if first in starts:
                copy(starts.index(first)).wait()
            all_got = []
            for n in range(first, first + 8):
                both = jnp.concatenate([blocks[n, 0], blocks[n, 1]], axis=1)
                all_got.append(jnp.dot(rows[k2_ref[n]], both, preferred_element_type=jnp.float32))
            for n in range(first, first + 8):
                k = k2_ref[n]
                got = all_got[n - first][:64] + all_got[n - first][64:]
                keep = mask_ref[pl.ds(k4_ref[n], 1), :]
                for r, ref in ((0, mine_ref), (32, theirs_ref)):
                    ref[0, k] = (got[r : r + 16, :128] - got[r + 16 : r + 32, 128:]) * keep
                    ref[1, k] = (got[r : r + 16, 128:] + got[r + 16 : r + 32, :128]) * keep

    result = jax.ShapeDtypeStruct((2, 64, 16, 128), jnp.float32)
    vmem = pl.BlockSpec(memory_space=pltpu.VMEM)
    return pl.pallas_call(
        kernel,
        in_specs=[pl.BlockSpec(memory_space=pltpu.SMEM)] * 2
        + [vmem] * 3
        + [pl.BlockSpec(memory_space=pltpu.HBM)] * len(held),
        out_specs=[vmem, vmem],
        out_shape=[result, result],
        scratch_shapes=[
            pltpu.VMEM((64, 2, 256, 128), jnp.bfloat16),
            pltpu.VMEM((64, 128, 256), jnp.bfloat16),
            pltpu.SemaphoreType.DMA((len(held),)),
        ],
        compiler_params=pltpu.CompilerParams(vmem_limit_bytes=18 * MIB),
        cost_estimate=LIGHT,
        name="contract_virtual",
    )(k4, k2, mask, u, pair, *held)


def per_device(ints, vir_coef, occ_coef, k4_table, band_mask):
    mom, band = lax.axis_index("mom"), lax.axis_index("band")
    core, y = band % 2, band // 2

    def across(x):
        return lax.ppermute(x, "band", [(i, i ^ 1) for i in range(8)])

    def along(x, d):
        return lax.ppermute(x, "band", [(i, (i // 2 + d) % 4 * 2 + i % 2) for i in range(8)])

    half = lax.dynamic_slice_in_dim(vir_coef, 128 * core, 128, axis=3)

    def onward(v, second, d):
        pairs = []
        for i in range(16):
            for j in range(8):
                to = (i // 4 + d) % 4 * 4 + i % 4 if (j % 2 == 1) != second else i // 4 * 4 + (i % 4 + d) % 4
                pairs.append((8 * i + j, 8 * to + j))
        return lax.ppermute(v, ("mom", "band"), pairs)

    offset = jnp.array([0, -1, 1, 2])
    n = jnp.arange(64)
    within, beyond, local = offset[n // 4 % 4], offset[n // 16], n % 4
    x = mom // 4 + jnp.where(core == 0, beyond, within)
    z = mom % 4 + jnp.where(core == 0, within, beyond)
    held_k4 = 4 * (4 * (x % 4) + z % 4) + local
    mask = lax.dynamic_slice_in_dim(band_mask, 128 * core, 128, axis=1).astype(jnp.float32)

    occ = lax.dynamic_slice_in_dim(occ_coef, 4 * mom, 4, axis=0)
    order = (
        2 * ((core + jnp.arange(2)[:, None, None]) % 2)
        + 4 * ((y + jnp.arange(4)[None, :, None]) % 4)
        + jnp.arange(2)[None, None, :]
    ).reshape(16)
    occ = jnp.take(occ, order, axis=3).reshape(4, 2, 32, 8, 2)
    parts = jnp.stack([jnp.stack([occ[:, 0], -occ[:, 1]], 1), jnp.stack([occ[:, 1], occ[:, 0]], 1)], 1)
    coef = parts.transpose(0, 4, 1, 5, 2, 3).reshape(4, 2, 16, 64)
    coef_own, coef_partner = coef[:, 0], coef[:, 1]

    ints = pltpu.with_memory_space_constraint(ints.reshape(2, 4, 16, 256, 256), pltpu.HBM)
    def after(x, *others):
        return lax.optimization_barrier((x, *others))[0]

    near = [onward(half, False, d) for d in (1, -1, 2)]
    row = jnp.concatenate([half, *near])
    below, above = onward(row, True, 1), onward(row, True, -1)
    chunks = range(0, 4, COUNT)
    partner = [contract_occupied(coef_partner, ints, first)[0] for first in chunks]
    arrived = [across(x) for x in partner]
    arrived[0] = after(arrived[0], row)
    sent = [contract_occupied(coef_own, ints, first, got) for first, got in zip(chunks, arrived)]
    owns, rights, lefts = [x[0] for x in sent], [x[1] for x in sent], [x[2] for x in sent]
    ups = along(jnp.concatenate([x[3] for x in sent], axis=1), 1)
    downs = [along(x[4], -1) for x in sent]
    right = (jnp.concatenate(rights, axis=1) + ups[:8].astype(jnp.float32)).astype(jnp.bfloat16)
    left = [(r + x[8:].astype(jnp.float32)).astype(jnp.bfloat16) for r, x in zip(lefts, downs)]
    left = jnp.concatenate(left, axis=1)
    low, high = lax.optimization_barrier((below[:8], above[8:], left))[:2]
    opposite = [onward(low, True, 1), onward(high, True, -1)]
    held = [row, below, above] + opposite
    owns[0] = after(owns[0], *opposite)
    coded = code_sums(owns, ups, downs, along(right, 1), along(left, -1), k4_table)
    u = lax.all_to_all(coded, "mom", split_axis=0, concat_axis=0, tiled=True)
    pair = across(u)
    k4 = u[:, 128, :4].astype(jnp.int32).reshape(64)
    k2 = jnp.sum(jnp.where(held_k4[:, None] == k4[None, :], n[None, :], 0), axis=1)
    held = [pltpu.with_memory_space_constraint(x, pltpu.HBM) for x in held]
    mine, theirs = contract_virtual(held_k4, k2, mask, held, u, pair)
    theirs = across(theirs)
    low, high = jnp.concatenate([mine, theirs], axis=-1), jnp.concatenate([theirs, mine], axis=-1)
    return jnp.where(core == 0, low, high).reshape(2, 64, 1, 2, 8, 256)


def solution(mesh):
    placed = (
        P(None, "mom", None, "band", None, None),
        P("mom", None, None, None),
        P(None, None, "band", None),
        P("mom", None),
        P(),
    )
    return jax.shard_map(
        per_device,
        mesh=mesh,
        in_specs=placed,
        out_specs=P(None, None, "mom", "band", None, None),
        check_vma=False,
    )
```

```python
import jax
import jax.numpy as jnp
from jax import lax
from jax.experimental import pallas as pl
from jax.experimental.pallas import tpu as pltpu
from jax.sharding import PartitionSpec as P

COUNT = 2
PAIR_TYPE = jnp.bfloat16
PIECE = 4
MIB = 1 << 20
LIGHT = pl.CostEstimate(flops=1, bytes_accessed=1, transcendentals=0)


def wide_rows(coef, wide):
    rows = lax.broadcasted_iota(jnp.int32, (128, 16), 0) // 8
    spread = (rows == lax.broadcasted_iota(jnp.int32, (128, 16), 1)).astype(jnp.bfloat16)
    cols = lax.broadcasted_iota(jnp.int32, (64, 512), 1) // 8
    across = (cols == lax.broadcasted_iota(jnp.int32, (64, 512), 0)).astype(jnp.bfloat16)
    same = lax.broadcasted_iota(jnp.int32, (128, 512), 0) % 8 == lax.broadcasted_iota(jnp.int32, (128, 512), 1) % 8
    tall = jnp.dot(spread, coef, preferred_element_type=jnp.float32).astype(jnp.bfloat16)
    full = jnp.dot(tall, across, preferred_element_type=jnp.float32)
    wide[...] = jnp.where(same, full, 0.0).astype(jnp.bfloat16)


def contract_occupied(coef, ints, first, got=None):
    def kernel(coef_ref, ints_ref, *rest):
        blocks, wide, sems = rest[-3:]
        refs = rest[:-3]

        def copy(c, p):
            return pltpu.make_async_copy(
                ints_ref.at[:, first + c, pl.ds(p * PIECE, PIECE)], blocks.at[c, p], sems.at[c, p]
            )

        for c in range(COUNT):
            for p in range(16 // PIECE):
                copy(c, p).start()
        for c in range(COUNT):
            wide_rows(coef_ref[first + c], wide.at[c])
        for c in range(COUNT):
            for p in range(16 // PIECE):
                copy(c, p).wait()
                for t in range(p * PIECE, p * PIECE + PIECE):
                    sums = jnp.dot(wide[c, :, :256], blocks[c, p, 0, t % PIECE], preferred_element_type=jnp.float32)
                    sums = sums + jnp.dot(
                        wide[c, :, 256:], blocks[c, p, 1, t % PIECE], preferred_element_type=jnp.float32
                    )
                    if got is None:
                        for d in range(4):
                            refs[0][d, t, c] = sums[32 * d : 32 * d + 32].astype(PAIR_TYPE)
                        continue
                    got_ref, own_ref, right_ref, left_ref, up_ref, down_ref = refs
                    total = [sums[32 * d : 32 * d + 32] + got_ref[d, t, c].astype(jnp.float32) for d in range(4)]
                    own_ref[t, c] = total[0]
                    if t < 8:
                        right_ref[t, c] = total[1]
                        up_ref[t, c] = total[2].astype(jnp.bfloat16)
                        down_ref[t, c] = total[3].astype(jnp.bfloat16)
                    else:
                        up_ref[t, c] = total[1].astype(jnp.bfloat16)
                        down_ref[t, c] = total[2].astype(jnp.bfloat16)
                        left_ref[t - 8, c] = total[3]

    vmem = pl.BlockSpec(memory_space=pltpu.VMEM)
    given, shapes = [coef, ints], [jax.ShapeDtypeStruct((4, 16, COUNT, 32, 256), PAIR_TYPE)]
    if got is not None:
        given.append(got)
        shapes = [
            jax.ShapeDtypeStruct((16, COUNT, 32, 256), jnp.float32),
            jax.ShapeDtypeStruct((8, COUNT, 32, 256), jnp.float32),
            jax.ShapeDtypeStruct((8, COUNT, 32, 256), jnp.float32),
            jax.ShapeDtypeStruct((16, COUNT, 32, 256), jnp.bfloat16),
            jax.ShapeDtypeStruct((16, COUNT, 32, 256), jnp.bfloat16),
        ]
    return pl.pallas_call(
        kernel,
        in_specs=[vmem, pl.BlockSpec(memory_space=pltpu.HBM)] + [vmem] * (len(given) - 2),
        out_specs=[vmem] * len(shapes),
        out_shape=shapes,
        scratch_shapes=[
            pltpu.VMEM((COUNT, 16 // PIECE, 2, PIECE, 256, 256), jnp.bfloat16),
            pltpu.VMEM((COUNT, 128, 512), jnp.bfloat16),
            pltpu.SemaphoreType.DMA((COUNT, 16 // PIECE)),
        ],
        compiler_params=pltpu.CompilerParams(vmem_limit_bytes=18 * MIB),
        cost_estimate=LIGHT,
        name="contract_partner" if got is None else "contract_own",
    )(*given)


def code_sums(owns, ups, downs, right, left, table):
    n = len(owns)

    def kernel(*refs):
        own_refs, down_refs = refs[:n], refs[n : 2 * n]
        up_ref, right_ref, left_ref, table_ref, out_ref = refs[2 * n :]
        line = lax.broadcasted_iota(jnp.int32, (16, 256), 0)
        lane = lax.broadcasted_iota(jnp.int32, (16, 256), 1)
        for t in range(16):
            extra = jnp.zeros((16, 256), jnp.int32)
            for k in range(4):
                i, c = k // COUNT, k % COUNT
                sums = own_refs[i][t, c] + (down_refs[i][t, c] if t < 8 else up_ref[t, k]).astype(jnp.float32)
                sums = sums + (right_ref[t, k] if t < 8 else left_ref[t - 8, k]).astype(jnp.float32)
                most = jnp.max(jnp.max(jnp.abs(sums), axis=0, keepdims=True), axis=1, keepdims=True)
                power = jnp.floor(jnp.log2(jnp.maximum(most, 1e-30))) + 1.0
                coded = jnp.floor(sums * jnp.exp2(14.5 - power) + 0.5).astype(jnp.int32)
                out_ref[t, 32 * k : 32 * k + 32] = coded.astype(jnp.int16)
                extra = jnp.where((line == 0) & (lane == k), table_ref[k, t], extra)
                extra = jnp.where(line == 1 + k, power.astype(jnp.int32), extra)
            out_ref[t, 128:144] = extra.astype(jnp.int16)

    vmem = pl.BlockSpec(memory_space=pltpu.VMEM)
    return pl.pallas_call(
        kernel,
        in_specs=[vmem] * (2 * n + 3) + [pl.BlockSpec(memory_space=pltpu.SMEM)],
        out_specs=vmem,
        out_shape=jax.ShapeDtypeStruct((16, 144, 256), jnp.int16),
        compiler_params=pltpu.CompilerParams(vmem_limit_bytes=18 * MIB),
        cost_estimate=LIGHT,
        name="code_sums",
    )(*owns, *downs, ups, right, left, table)


def contract_virtual(k4, k2, mask, held, u, pair):
    sizes = [x.shape[0] for x in held]
    starts = [sum(sizes[:i]) for i in range(len(held))]

    def kernel(k4_ref, k2_ref, mask_ref, u_ref, pair_ref, *rest):
        held_refs, (mine_ref, theirs_ref, blocks, rows, sems) = rest[: len(held)], rest[len(held) :]

        def copy(i):
            return pltpu.make_async_copy(held_refs[i], blocks.at[pl.ds(starts[i], sizes[i])], sems.at[i])

        for i in range(len(held)):
            copy(i).start()

        for j in range(16):
            for h, ref in enumerate((u_ref, pair_ref)):
                scale = jnp.exp2(ref[j, 128:144].astype(jnp.int32).astype(jnp.float32) - 14.5)
                for c in range(4):
                    full = ref[j, 32 * c : 32 * c + 32].astype(jnp.int32).astype(jnp.float32) * scale[1 + c : 2 + c]
                    high = full.astype(jnp.bfloat16)
                    low = (full - high.astype(jnp.float32)).astype(jnp.bfloat16)
                    rows[4 * j + c, 32 * h : 32 * h + 32] = high
                    rows[4 * j + c, 64 + 32 * h : 96 + 32 * h] = low

        for first in range(0, 64, 8):
            if first in starts:
                copy(starts.index(first)).wait()
            all_got = []
            for n in range(first, first + 8):
                both = jnp.concatenate([blocks[n, 0], blocks[n, 1]], axis=1)
                all_got.append(jnp.dot(rows[k2_ref[n]], both, preferred_element_type=jnp.float32))
            for n in range(first, first + 8):
                k = k2_ref[n]
                got = all_got[n - first][:64] + all_got[n - first][64:]
                keep = mask_ref[pl.ds(k4_ref[n], 1), :]
                for r, ref in ((0, mine_ref), (32, theirs_ref)):
                    ref[0, k] = (got[r : r + 16, :128] - got[r + 16 : r + 32, 128:]) * keep
                    ref[1, k] = (got[r : r + 16, 128:] + got[r + 16 : r + 32, :128]) * keep

    result = jax.ShapeDtypeStruct((2, 64, 16, 128), jnp.float32)
    vmem = pl.BlockSpec(memory_space=pltpu.VMEM)
    return pl.pallas_call(
        kernel,
        in_specs=[pl.BlockSpec(memory_space=pltpu.SMEM)] * 2
        + [vmem] * 3
        + [pl.BlockSpec(memory_space=pltpu.HBM)] * len(held),
        out_specs=[vmem, vmem],
        out_shape=[result, result],
        scratch_shapes=[
            pltpu.VMEM((64, 2, 256, 128), jnp.bfloat16),
            pltpu.VMEM((64, 128, 256), jnp.bfloat16),
            pltpu.SemaphoreType.DMA((len(held),)),
        ],
        compiler_params=pltpu.CompilerParams(vmem_limit_bytes=18 * MIB),
        cost_estimate=LIGHT,
        name="contract_virtual",
    )(k4, k2, mask, u, pair, *held)


def per_device(ints, vir_coef, occ_coef, k4_table, band_mask):
    mom, band = lax.axis_index("mom"), lax.axis_index("band")
    core, y = band % 2, band // 2

    def across(x):
        return lax.ppermute(x, "band", [(i, i ^ 1) for i in range(8)])

    def along(x, d):
        return lax.ppermute(x, "band", [(i, (i // 2 + d) % 4 * 2 + i % 2) for i in range(8)])

    half = lax.dynamic_slice_in_dim(vir_coef, 128 * core, 128, axis=3)

    def onward(v, second, d):
        pairs = []
        for i in range(16):
            for j in range(8):
                to = (i // 4 + d) % 4 * 4 + i % 4 if (j % 2 == 1) != second else i // 4 * 4 + (i % 4 + d) % 4
                pairs.append((8 * i + j, 8 * to + j))
        return lax.ppermute(v, ("mom", "band"), pairs)

    offset = jnp.array([0, -1, 1, 2])
    n = jnp.arange(64)
    within, beyond, local = offset[n // 4 % 4], offset[n // 16], n % 4
    x = mom // 4 + jnp.where(core == 0, beyond, within)
    z = mom % 4 + jnp.where(core == 0, within, beyond)
    held_k4 = 4 * (4 * (x % 4) + z % 4) + local
    mask = lax.dynamic_slice_in_dim(band_mask, 128 * core, 128, axis=1).astype(jnp.float32)

    occ = lax.dynamic_slice_in_dim(occ_coef, 4 * mom, 4, axis=0)
    order = (
        2 * ((core + jnp.arange(2)[:, None, None]) % 2)
        + 4 * ((y + jnp.arange(4)[None, :, None]) % 4)
        + jnp.arange(2)[None, None, :]
    ).reshape(16)
    occ = jnp.take(occ, order, axis=3).reshape(4, 2, 32, 8, 2)
    parts = jnp.stack([jnp.stack([occ[:, 0], -occ[:, 1]], 1), jnp.stack([occ[:, 1], occ[:, 0]], 1)], 1)
    coef = parts.transpose(0, 4, 1, 5, 2, 3).reshape(4, 2, 16, 64)
    coef_own, coef_partner = coef[:, 0], coef[:, 1]

    ints = pltpu.with_memory_space_constraint(ints.reshape(2, 4, 16, 256, 256), pltpu.HBM)
    def after(x, *others):
        return lax.optimization_barrier((x, *others))[0]

    near = [onward(half, False, d) for d in (1, -1, 2)]
    row = jnp.concatenate([half, *near])
    below, above = onward(row, True, 1), onward(row, True, -1)
    chunks = range(0, 4, COUNT)
    partner = [contract_occupied(coef_partner, ints, first)[0] for first in chunks]
    arrived = [across(x) for x in partner]
    arrived[0] = after(arrived[0], row)
    sent = [contract_occupied(coef_own, ints, first, got) for first, got in zip(chunks, arrived)]
    owns, rights, lefts = [x[0] for x in sent], [x[1] for x in sent], [x[2] for x in sent]
    ups = along(jnp.concatenate([x[3] for x in sent], axis=1), 1)
    downs = [along(x[4], -1) for x in sent]
    right = (jnp.concatenate(rights, axis=1) + ups[:8].astype(jnp.float32)).astype(jnp.bfloat16)
    left = [(r + x[8:].astype(jnp.float32)).astype(jnp.bfloat16) for r, x in zip(lefts, downs)]
    left = jnp.concatenate(left, axis=1)
    low, high = lax.optimization_barrier((below[:8], above[8:], left))[:2]
    opposite = [onward(low, True, 1), onward(high, True, -1)]
    held = [row, below, above] + opposite
    owns[0] = after(owns[0], *opposite)
    coded = code_sums(owns, ups, downs, along(right, 1), along(left, -1), k4_table)
    u = lax.all_to_all(coded, "mom", split_axis=0, concat_axis=0, tiled=True)
    pair = across(u)
    k4 = u[:, 128, :4].astype(jnp.int32).reshape(64)
    k2 = jnp.sum(jnp.where(held_k4[:, None] == k4[None, :], n[None, :], 0), axis=1)
    held = [pltpu.with_memory_space_constraint(x, pltpu.HBM) for x in held]
    mine, theirs = contract_virtual(held_k4, k2, mask, held, u, pair)
    theirs = across(theirs)
    low, high = jnp.concatenate([mine, theirs], axis=-1), jnp.concatenate([theirs, mine], axis=-1)
    return jnp.where(core == 0, low, high).reshape(2, 64, 1, 2, 8, 256)


def solution(mesh):
    placed = (
        P(None, "mom", None, "band", None, None),
        P("mom", None, None, None),
        P(None, None, "band", None),
        P("mom", None),
        P(),
    )
    return jax.shard_map(
        per_device,
        mesh=mesh,
        in_specs=placed,
        out_specs=P(None, None, "mom", "band", None, None),
        check_vma=False,
    )
```
